256 devices in a mesh: space: 64 (over x, z_lo, y), chan: 4 (over z_hi, core).
Axes of the slice: x: 4, y: 4, z: 8 (z_hi: 2, z_lo: 4; z = z_hi * 4 + z_lo), core: 2. Of those that a mesh axis runs over, the one named last changes fastest.
Arguments:
- inputs: float32 [128, 8, 128, 128], P('chan', None, 'space'), may hold values from -6 to 6
- out_grad: float32 [128, 8, 128, 128], P('chan', None, 'space'), may hold values from -6 to 6
- weights: float32 [3, 3, 3, 128, 128], P(None, None, None, 'chan'), may hold values from -0.109375 to 0.109375
Outputs:
- input_grad: float32 [128, 8, 128, 128], P('chan', None, 'space')
- weight_grad: float32 [3, 3, 3, 128, 128], P(None, None, None, 'chan')
The draws below stay inside these ranges and needn't reach their ends.
All inputs are finite; a program needn't handle non-finite values.
Results may differ from the reference program's by a relative error of at most 0.00025.
Values sent between devices are 32-bit elements; how exact they have to be, the bound alone decides.
No kernel may reach another device: no remote copies, remote signals or barrier semaphores. Data moves between devices by JAX's collectives and lax.ppermute only.
A program may use at most 192 MiB of HBM per device.

```python
import jax
import jax.numpy as jnp
from jax import lax

CHANNELS = 128
FILTERS = 128
PLANES = 8
COLS = 128
ROWS = 128


def level_of(key, shape, split, smallest, largest):
    factor_of = 1.0
    for dim, blocks in split:
        draws = jax.random.uniform(jax.random.fold_in(jax.random.fold_in(key, 6), dim), (blocks,), jnp.float32, smallest / len(split), largest / len(split))
        factor_of = factor_of * jnp.repeat(jnp.exp(draws), shape[dim] // blocks).reshape((-1,) + (1,) * (len(shape) - 1 - dim))
    return factor_of


def normal_values(stream_key, shape, width, limit, pieces=(), kind=jnp.bfloat16):
    entries = jax.random.normal(stream_key, shape, jnp.float32) * width
    if len(pieces) > 0:
        entries = level_of(stream_key, shape, pieces, -0.22, 0.18) * entries
    return jnp.clip(entries, min=-limit, max=limit).astype(kind)


def setup_inputs(seed: int = 0) -> dict:
    keys = jax.random.split(jax.random.key(seed), 4)
    return {
        "inputs": normal_values(keys[0], (CHANNELS, PLANES, ROWS, COLS), 1.0, 6.0, ((0, 4), (2, 64)), jnp.float32),
        "out_grad": normal_values(keys[1], (FILTERS, PLANES, ROWS, COLS), 1.0, 6.0, ((0, 4), (2, 64)), jnp.float32),
        "weights": normal_values(keys[2], (3, 3, 3, CHANNELS, FILTERS), (27 * FILTERS) ** -0.5, 0.109375, ((3, 4),), jnp.float32),
    }


def reference(inputs, out_grad, weights):
    kernel = jnp.transpose(weights, (4, 3, 0, 1, 2))

    def forward(volume, taps):
        return lax.conv_general_dilated(volume[None], taps, (1, 1, 1), 'SAME', dimension_numbers=('NCDHW', 'OIDHW', 'NCDHW'), precision=lax.Precision.HIGHEST)[0]
    _, pullback = jax.vjp(forward, inputs, kernel)
    input_grad, kernel_grad = pullback(out_grad)
    normalizer = 1.0 / jnp.sqrt(jnp.float32(PLANES * ROWS * COLS))
    weight_grad = jnp.transpose(kernel_grad, (2, 3, 4, 1, 0)) * normalizer
    return (input_grad, weight_grad)
```

```python
import math

import jax
import jax.numpy as jnp
from jax import lax
from jax.experimental import pallas as pl
from jax.experimental.pallas import tpu as pltpu
from jax.sharding import PartitionSpec as P

BF = jnp.bfloat16
F32 = jnp.float32


def split(value):
    high = value.astype(BF)
    return high, (value - high.astype(F32)).astype(BF)


def shifted(value, step):
    lanes = value.shape[1]
    lane = lax.broadcasted_iota(jnp.int32, value.shape, 1)
    edge = lanes - 1 if step > 0 else 0
    return jnp.where(lane == edge, 0.0, pltpu.roll(value, (-step) % lanes, 1))


def load_grads(parts, grads, chan):
    filters = grads.shape[0] // 2
    count = filters // len(parts)
    pairs = parts[0].shape[0] // count
    for j, part in enumerate(parts):
        start = pl.multiple_of((chan ^ j) * count, count)
        for r in range(pairs):
            high, low = split(part[pl.ds(r, count, stride=pairs), :])
            grads[pl.ds(start, count), r * 128 : (r + 1) * 128] = high
            grads[pl.ds(filters + start, count), r * 128 : (r + 1) * 128] = low


def weight_kernel(scale, planes, x, above, below, g0, g1, g2, g3, out, cells, grads):
    chan = lax.axis_index("chan")
    load_grads((g0, g1, g2, g3), grads, chan)
    count = x.shape[0] // (2 * planes)
    filters = grads.shape[0] // 2
    cells[:, : 4 * 128] = jnp.zeros((cells.shape[0], 4 * 128), BF)
    cells[:, (planes + 1) * 512 :] = jnp.zeros((cells.shape[0], 512), BF)
    for d in range(planes):
        for r in range(4):
            if r == 0:
                value = above[pl.ds(d, count, stride=planes), :]
            elif r == 3:
                value = below[pl.ds(d, count, stride=planes), :]
            else:
                value = x[pl.ds(2 * d + r - 1, count, stride=2 * planes), :]
            at = ((d + 1) * 4 + r) * 128
            for kw in range(3):
                moved = value if kw == 1 else shifted(value, kw - 1)
                high, low = split(moved)
                cells[kw * 2 * count : (kw * 2 + 1) * count, at : at + 128] = high
                cells[(kw * 2 + 1) * count : (kw * 2 + 2) * count, at : at + 128] = low
    for kd in range(3):
        for kh in range(3):
            left = jnp.concatenate(
                [
                    cells[:, ((d + kd) * 4 + kh) * 128 : ((d + kd) * 4 + kh) * 128 + 256]
                    for d in range(planes)
                ],
                axis=1,
            )
            full = lax.dot_general(
                left, grads[...], (((1,), (1,)), ((), ())), preferred_element_type=F32
            )
            for kw in range(3):
                high = full[kw * 2 * count : (kw * 2 + 1) * count]
                low = full[(kw * 2 + 1) * count : (kw * 2 + 2) * count]
                total = high[:, :filters] + (high[:, filters:] + low[:, :filters])
                tap = (kd * 3 + kh) * 3 + kw
                out[tap * count : (tap + 1) * count, :] = total * scale


def input_kernel(planes, w, g0, g1, g2, g3, out, above, below, left, grads):
    chan = lax.axis_index("chan")
    load_grads((g0, g1, g2, g3), grads, chan)
    count = w.shape[0] // 27
    filters = grads.shape[0] // 2
    block = 9 * count
    for kd in range(3):
        high, low = split(w[kd * block : (kd + 1) * block, :])
        left[:, (kd * 3) * filters : (kd * 3 + 1) * filters] = high
        left[:, (kd * 3 + 1) * filters : (kd * 3 + 2) * filters] = low
        left[:, (kd * 3 + 2) * filters : (kd * 3 + 3) * filters] = high
    for q in range(planes):
        taps = [kd for kd in range(3) if 0 <= q - kd + 1 < planes]
        right = []
        for kd in taps:
            d = q - kd + 1
            high = grads[:filters, d * 256 : (d + 1) * 256]
            right += [high, high, grads[filters:, d * 256 : (d + 1) * 256]]
        full = jnp.dot(
            left[:, taps[0] * 3 * filters : (taps[-1] + 1) * 3 * filters],
            jnp.concatenate(right, axis=0),
            preferred_element_type=F32,
        )

        def term(kh, kw, h):
            at = (kh * 3 + kw) * count
            return full[at : at + count, h * 128 : (h + 1) * 128]

        def row(pairs):
            sums = []
            for kw in range(3):
                values = [term(kh, kw, h) for kh, h in pairs]
                sums.append(sum(values[1:], values[0]))
            return shifted(sums[0], 1) + sums[1] + shifted(sums[2], -1)

        out[pl.ds(2 * q, count, stride=2 * planes), :] = row([(1, 0), (0, 1)])
        out[pl.ds(2 * q + 1, count, stride=2 * planes), :] = row([(2, 0), (1, 1)])
        above[pl.ds(q, count, stride=planes), :] = row([(0, 0)])
        below[pl.ds(q, count, stride=planes), :] = row([(2, 1)])


AXES = 4


def place(deltas):
    pairs = []
    for i in range(AXES**3):
        x, z, y = i // (AXES * AXES), (i // AXES) % AXES, i % AXES
        pairs.append((i, ((x ^ deltas[0]) * AXES + (z ^ deltas[1])) * AXES + (y ^ deltas[2])))
    return pairs


def toward(axis, step):
    deltas = [0, 0, 0]
    deltas[axis] = step
    return place(deltas)


def sum_over_space(value):
    me = lax.axis_index("space")
    last = me % AXES
    length = value.shape[0] // AXES

    def piece(index):
        return lax.dynamic_slice_in_dim(value, index * length, length, 0)

    total = piece(last)
    for k in (1, 2, 3):
        total = total + lax.ppermute(piece(last ^ k), "space", toward(2, k))
    for axis in (0, 1):
        held = total
        for k in (1, 2, 3):
            total = total + lax.ppermute(held, "space", toward(axis, k))
    parts = [total] + [lax.ppermute(total, "space", toward(2, k)) for k in (1, 2, 3)]
    result = jnp.zeros(value.shape, value.dtype)
    for k in range(4):
        result = lax.dynamic_update_slice_in_dim(result, parts[k], (last ^ k) * length, 0)
    return result


def per_device(inputs, out_grad, weights):
    channels, planes, rows, cols = inputs.shape
    filters = weights.shape[4]
    cell_total = planes * rows * lax.axis_size("space") * cols
    scale = 1.0 / math.sqrt(cell_total)
    x = inputs.reshape(-1, cols)
    g0 = out_grad.reshape(-1, cols)
    w = weights.reshape(-1, filters)
    peers = lax.axis_size("space")
    up = [(i, i + 1) for i in range(peers - 1)]
    down = [(j, i) for i, j in up]
    g2 = lax.ppermute(g0, "chan", [(i, i ^ 2) for i in range(4)])
    g1 = lax.ppermute(g0, "chan", [(i, i ^ 1) for i in range(4)])
    above = lax.ppermute(inputs[:, :, 1, :].reshape(-1, cols), "space", up)
    below = lax.ppermute(inputs[:, :, 0, :].reshape(-1, cols), "space", down)
    g3 = lax.ppermute(g2, "chan", [(i, i ^ 1) for i in range(4)])
    cells = planes * rows * cols

    def vmem(n):
        return [pl.BlockSpec(memory_space=pltpu.VMEM)] * n

    partial = pl.pallas_call(
        lambda *refs: weight_kernel(scale, planes, *refs),
        out_shape=jax.ShapeDtypeStruct((27 * channels, filters), F32),
        in_specs=vmem(7),
        out_specs=vmem(1)[0],
        scratch_shapes=[
            pltpu.VMEM((6 * channels, (planes + 2) * 4 * cols), BF),
            pltpu.VMEM((2 * filters, cells), BF),
        ],
        compiler_params=pltpu.CompilerParams(vmem_limit_bytes=48 * 1024 * 1024),
        cost_estimate=pl.CostEstimate(
            flops=6 * 27 * channels * filters * cells, bytes_accessed=2**21, transcendentals=0
        ),
        name="weight_kernel",
    )(x, above, below, g0, g1, g2, g3)
    halo = jax.ShapeDtypeStruct((channels * planes, cols), F32)
    core, to_above, to_below = pl.pallas_call(
        lambda *refs: input_kernel(planes, *refs),
        out_shape=(jax.ShapeDtypeStruct(x.shape, F32), halo, halo),
        in_specs=vmem(5),
        out_specs=tuple(vmem(3)),
        scratch_shapes=[
            pltpu.VMEM((9 * channels, 9 * filters), BF),
            pltpu.VMEM((2 * filters, cells), BF),
        ],
        compiler_params=pltpu.CompilerParams(vmem_limit_bytes=48 * 1024 * 1024),
        cost_estimate=pl.CostEstimate(
            flops=6 * 27 * channels * filters * cells, bytes_accessed=2**21, transcendentals=0
        ),
        name="input_kernel",
    )(w, g0, g1, g2, g3)
    from_above = lax.ppermute(to_below, "space", up).reshape(channels, planes, cols)
    from_below = lax.ppermute(to_above, "space", down).reshape(channels, planes, cols)
    input_grad = core.reshape(inputs.shape) + jnp.stack([from_above, from_below], axis=2)
    weight_grad = sum_over_space(partial).reshape(3, 3, 3, channels, filters)
    return (input_grad, weight_grad)


def solution(mesh):
    return jax.shard_map(
        per_device,
        mesh=mesh,
        in_specs=(
            P("chan", None, "space", None),
            P("chan", None, "space", None),
            P(None, None, None, "chan", None),
        ),
        out_specs=(P("chan", None, "space", None), P(None, None, None, "chan", None)),
        check_vma=False,
    )
```

```python
import math

import jax
import jax.numpy as jnp
from jax import lax
from jax.experimental import pallas as pl
from jax.experimental.pallas import tpu as pltpu
from jax.sharding import PartitionSpec as P

BF = jnp.bfloat16
F32 = jnp.float32


def split(value):
    high = value.astype(BF)
    return high, (value - high.astype(F32)).astype(BF)


def shifted(value, step):
    lanes = value.shape[1]
    lane = lax.broadcasted_iota(jnp.int32, value.shape, 1)
    edge = lanes - 1 if step > 0 else 0
    return jnp.where(lane == edge, 0.0, pltpu.roll(value, (-step) % lanes, 1))


def load_grads(parts, grads, chan):
    filters = grads.shape[0] // 2
    count = filters // len(parts)
    pairs = parts[0].shape[0] // count
    for j, part in enumerate(parts):
        start = pl.multiple_of((chan ^ j) * count, count)
        for r in range(pairs):
            high, low = split(part[pl.ds(r, count, stride=pairs), :])
            grads[pl.ds(start, count), r * 128 : (r + 1) * 128] = high
            grads[pl.ds(filters + start, count), r * 128 : (r + 1) * 128] = low


def weight_kernel(scale, planes, x, near, far, g0, g1, g2, g3, out, cells, grads):
    chan = lax.axis_index("chan")
    load_grads((g0, g1, g2, g3), grads, chan)
    count = x.shape[0] // (2 * planes)
    filters = grads.shape[0] // 2
    cells[:, : 4 * 128] = jnp.zeros((cells.shape[0], 4 * 128), BF)
    cells[:, (planes + 1) * 512 :] = jnp.zeros((cells.shape[0], 512), BF)
    odd = lax.axis_index("space") % 2 == 1
    for d in range(planes):
        for r in range(4):
            if r in (0, 3):
                inner = near[pl.ds(d, count, stride=planes), :]
                outer = far[pl.ds(d, count, stride=planes), :]
                value = jnp.where(odd, inner, outer) if r == 0 else jnp.where(odd, outer, inner)
            else:
                value = x[pl.ds(2 * d + r - 1, count, stride=2 * planes), :]
            at = ((d + 1) * 4 + r) * 128
            for kw in range(3):
                moved = value if kw == 1 else shifted(value, kw - 1)
                high, low = split(moved)
                cells[kw * 2 * count : (kw * 2 + 1) * count, at : at + 128] = high
                cells[(kw * 2 + 1) * count : (kw * 2 + 2) * count, at : at + 128] = low
    for kd in range(3):
        for kh in range(3):
            left = jnp.concatenate(
                [
                    cells[:, ((d + kd) * 4 + kh) * 128 : ((d + kd) * 4 + kh) * 128 + 256]
                    for d in range(planes)
                ],
                axis=1,
            )
            full = lax.dot_general(
                left, grads[...], (((1,), (1,)), ((), ())), preferred_element_type=F32
            )
            for kw in range(3):
                high = full[kw * 2 * count : (kw * 2 + 1) * count]
                low = full[(kw * 2 + 1) * count : (kw * 2 + 2) * count]
                total = high[:, :filters] + (high[:, filters:] + low[:, :filters])
                tap = (kd * 3 + kh) * 3 + kw
                out[tap * count : (tap + 1) * count, :] = total * scale


def input_kernel(planes, w, g0, g1, g2, g3, out, above, below, left, grads):
    chan = lax.axis_index("chan")
    load_grads((g0, g1, g2, g3), grads, chan)
    count = w.shape[0] // 27
    filters = grads.shape[0] // 2
    block = 9 * count
    for kd in range(3):
        high, low = split(w[kd * block : (kd + 1) * block, :])
        left[:, (kd * 3) * filters : (kd * 3 + 1) * filters] = high
        left[:, (kd * 3 + 1) * filters : (kd * 3 + 2) * filters] = low
        left[:, (kd * 3 + 2) * filters : (kd * 3 + 3) * filters] = high
    for q in range(planes):
        taps = [kd for kd in range(3) if 0 <= q - kd + 1 < planes]
        right = []
        for kd in taps:
            d = q - kd + 1
            high = grads[:filters, d * 256 : (d + 1) * 256]
            right += [high, high, grads[filters:, d * 256 : (d + 1) * 256]]
        full = jnp.dot(
            left[:, taps[0] * 3 * filters : (taps[-1] + 1) * 3 * filters],
            jnp.concatenate(right, axis=0),
            preferred_element_type=F32,
        )

        def term(kh, kw, h):
            at = (kh * 3 + kw) * count
            return full[at : at + count, h * 128 : (h + 1) * 128]

        def row(pairs):
            sums = []
            for kw in range(3):
                values = [term(kh, kw, h) for kh, h in pairs]
                sums.append(sum(values[1:], values[0]))
            return shifted(sums[0], 1) + sums[1] + shifted(sums[2], -1)

        out[pl.ds(2 * q, count, stride=2 * planes), :] = row([(1, 0), (0, 1)])
        out[pl.ds(2 * q + 1, count, stride=2 * planes), :] = row([(2, 0), (1, 1)])
        above[pl.ds(q, count, stride=planes), :] = row([(0, 0)])
        below[pl.ds(q, count, stride=planes), :] = row([(2, 1)])


AXES = 4


def groups_over_xy():
    return [
        [(x * AXES + z) * AXES + y for x in range(AXES) for y in range(AXES)] for z in range(AXES)
    ]


def z_pairs(step):
    return [(i, i ^ (step * AXES)) for i in range(AXES**3)]


def scattered(value):
    return lax.all_to_all(value, "space", 0, 0, axis_index_groups=groups_over_xy()).sum(axis=0)


def summed_over_z(value):
    total = value
    for step in (1, 2, 3):
        total = total + lax.ppermute(value, "space", z_pairs(step))
    return total


def gathered(value):
    pieces = jnp.broadcast_to(value[None], (AXES * AXES,) + value.shape)
    return lax.all_to_all(pieces, "space", 0, 0, axis_index_groups=groups_over_xy())


def swap_halo(first, last):
    count = lax.axis_size("space")
    odd = lax.axis_index("space") % 2 == 1
    inner = [(i, i ^ 1) for i in range(count)]
    outer = [(i, i + 1) for i in range(1, count - 1, 2)]
    outer = outer + [(j, i) for i, j in outer]
    a = lax.ppermute(jnp.where(odd, first, last), "space", inner)
    b = lax.ppermute(jnp.where(odd, last, first), "space", outer)
    return a, b, odd


def per_device(inputs, out_grad, weights):
    channels, planes, rows, cols = inputs.shape
    filters = weights.shape[4]
    cell_total = planes * rows * lax.axis_size("space") * cols
    scale = 1.0 / math.sqrt(cell_total)
    x = inputs.reshape(-1, cols)
    g0 = out_grad.reshape(-1, cols)
    w = weights.reshape(-1, filters)
    across = [(i, i ^ 2) for i in range(4)]
    beside = [(i, i ^ 1) for i in range(4)]
    g2 = lax.ppermute(g0, "chan", across)
    g1 = lax.ppermute(g0, "chan", beside)
    near, far, odd = swap_halo(
        inputs[:, :, 0, :].reshape(-1, cols), inputs[:, :, 1, :].reshape(-1, cols)
    )
    g1, g2, near, far = lax.optimization_barrier((g1, g2, near, far))
    g3 = lax.ppermute(g2, "chan", beside)
    cells = planes * rows * cols

    def vmem(n):
        return [pl.BlockSpec(memory_space=pltpu.VMEM)] * n

    partial = pl.pallas_call(
        lambda *refs: weight_kernel(scale, planes, *refs),
        out_shape=jax.ShapeDtypeStruct((27 * channels, filters), F32),
        in_specs=vmem(7),
        out_specs=vmem(1)[0],
        scratch_shapes=[
            pltpu.VMEM((6 * channels, (planes + 2) * 4 * cols), BF),
            pltpu.VMEM((2 * filters, cells), BF),
        ],
        compiler_params=pltpu.CompilerParams(vmem_limit_bytes=48 * 1024 * 1024),
        cost_estimate=pl.CostEstimate(
            flops=6 * 27 * channels * filters * cells, bytes_accessed=2**21, transcendentals=0
        ),
        name="weight_kernel",
    )(x, near, far, g0, g1, g2, g3)
    partial, w, g0, g1, g2, g3 = lax.optimization_barrier((partial, w, g0, g1, g2, g3))
    piece = scattered(partial.reshape(AXES * AXES, -1, 2, filters))
    halo = jax.ShapeDtypeStruct((channels * planes, cols), F32)
    core, to_above, to_below = pl.pallas_call(
        lambda *refs: input_kernel(planes, *refs),
        out_shape=(jax.ShapeDtypeStruct(x.shape, F32), halo, halo),
        in_specs=vmem(5),
        out_specs=tuple(vmem(3)),
        scratch_shapes=[
            pltpu.VMEM((9 * channels, 9 * filters), BF),
            pltpu.VMEM((2 * filters, cells), BF),
        ],
        compiler_params=pltpu.CompilerParams(vmem_limit_bytes=48 * 1024 * 1024),
        cost_estimate=pl.CostEstimate(
            flops=6 * 27 * channels * filters * cells, bytes_accessed=2**21, transcendentals=0
        ),
        name="input_kernel",
    )(w, g0, g1, g2, g3)
    near, far, odd = swap_halo(to_above, to_below)
    weight_grad = gathered(summed_over_z(piece))
    near = near.reshape(channels, planes, cols)
    far = far.reshape(channels, planes, cols)
    rims = jnp.stack([jnp.where(odd, near, far), jnp.where(odd, far, near)], axis=2)
    input_grad = core.reshape(inputs.shape) + rims
    weight_grad = weight_grad.reshape(3, 3, 3, channels, filters)
    return (input_grad, weight_grad)


def solution(mesh):
    return jax.shard_map(
        per_device,
        mesh=mesh,
        in_specs=(
            P("chan", None, "space", None),
            P("chan", None, "space", None),
            P(None, None, None, "chan", None),
        ),
        out_specs=(P("chan", None, "space", None), P(None, None, None, "chan", None)),
        check_vma=False,
    )
```

```python
import math

import jax
import jax.numpy as jnp
from jax import lax
from jax.experimental import pallas as pl
from jax.experimental.pallas import tpu as pltpu
from jax.sharding import PartitionSpec as P

BF = jnp.bfloat16
F32 = jnp.float32


def split(value):
    high = value.astype(BF)
    return high, (value - high.astype(F32)).astype(BF)


def shifted(value, step):
    lanes = value.shape[1]
    lane = lax.broadcasted_iota(jnp.int32, value.shape, 1)
    edge = lanes - 1 if step > 0 else 0
    return jnp.where(lane == edge, 0.0, pltpu.roll(value, (-step) % lanes, 1))


def load_grads(parts, grads, chan):
    filters = grads.shape[0] // 2
    count = filters // len(parts)
    pairs = parts[0].shape[0] // count
    for j, part in enumerate(parts):
        start = pl.multiple_of((chan ^ j) * count, count)
        for r in range(pairs):
            high, low = split(part[pl.ds(r, count, stride=pairs), :])
            grads[pl.ds(start, count), r * 128 : (r + 1) * 128] = high
            grads[pl.ds(filters + start, count), r * 128 : (r + 1) * 128] = low


def weight_kernel(scale, planes, x, near, far, g0, g1, g2, g3, out, cells, grads):
    chan = lax.axis_index("chan")
    load_grads((g0, g1, g2, g3), grads, chan)
    count = x.shape[0] // (2 * planes)
    filters = grads.shape[0] // 2
    cells[:, : 4 * 128] = jnp.zeros((cells.shape[0], 4 * 128), BF)
    cells[:, (planes + 1) * 512 :] = jnp.zeros((cells.shape[0], 512), BF)
    odd = lax.axis_index("space") % 2 == 1
    for d in range(planes):
        for r in range(4):
            if r in (0, 3):
                inner = near[pl.ds(d, count, stride=planes), :]
                outer = far[pl.ds(d, count, stride=planes), :]
                value = jnp.where(odd, inner, outer) if r == 0 else jnp.where(odd, outer, inner)
            else:
                value = x[pl.ds(2 * d + r - 1, count, stride=2 * planes), :]
            at = ((d + 1) * 4 + r) * 128
            for kw in range(3):
                moved = value if kw == 1 else shifted(value, kw - 1)
                high, low = split(moved)
                cells[kw * 2 * count : (kw * 2 + 1) * count, at : at + 128] = high
                cells[(kw * 2 + 1) * count : (kw * 2 + 2) * count, at : at + 128] = low
    for kh in range(3):
        stripes = []
        for kd in range(3):
            starts = [((d + kd) * 4 + kh) * 128 for d in range(planes)]
            stripes.append(jnp.concatenate([cells[:, i : i + 256] for i in starts], axis=1))
        full = lax.dot_general(
            jnp.concatenate(stripes, axis=0),
            grads[...],
            (((1,), (1,)), ((), ())),
            preferred_element_type=F32,
        )
        for kd in range(3):
            for kw in range(3):
                at = (kd * 3 + kw) * 2 * count
                high = full[at : at + count]
                low = full[at + count : at + 2 * count]
                total = high[:, :filters] + (high[:, filters:] + low[:, :filters])
                tap = (kd * 3 + kh) * 3 + kw
                out[tap * count : (tap + 1) * count, :] = total * scale


def input_kernel(planes, w, g0, g1, g2, g3, out, above, below, left, grads):
    chan = lax.axis_index("chan")
    load_grads((g0, g1, g2, g3), grads, chan)
    count = w.shape[0] // 27
    filters = grads.shape[0] // 2
    block = 9 * count
    for kd in range(3):
        high, low = split(w[kd * block : (kd + 1) * block, :])
        left[:, (kd * 3) * filters : (kd * 3 + 1) * filters] = high
        left[:, (kd * 3 + 1) * filters : (kd * 3 + 2) * filters] = low
        left[:, (kd * 3 + 2) * filters : (kd * 3 + 3) * filters] = high
    for q in range(planes):
        taps = [kd for kd in range(3) if 0 <= q - kd + 1 < planes]
        right = []
        for kd in taps:
            d = q - kd + 1
            high = grads[:filters, d * 256 : (d + 1) * 256]
            right += [high, high, grads[filters:, d * 256 : (d + 1) * 256]]
        full = jnp.dot(
            left[:, taps[0] * 3 * filters : (taps[-1] + 1) * 3 * filters],
            jnp.concatenate(right, axis=0),
            preferred_element_type=F32,
        )

        def term(kh, kw, h):
            at = (kh * 3 + kw) * count
            return full[at : at + count, h * 128 : (h + 1) * 128]

        def row(pairs):
            sums = []
            for kw in range(3):
                values = [term(kh, kw, h) for kh, h in pairs]
                sums.append(sum(values[1:], values[0]))
            return shifted(sums[0], 1) + sums[1] + shifted(sums[2], -1)

        out[pl.ds(2 * q, count, stride=2 * planes), :] = row([(1, 0), (0, 1)])
        out[pl.ds(2 * q + 1, count, stride=2 * planes), :] = row([(2, 0), (1, 1)])
        above[pl.ds(q, count, stride=planes), :] = row([(0, 0)])
        below[pl.ds(q, count, stride=planes), :] = row([(2, 1)])


AXES = 4


def groups_over_xy():
    return [
        [(x * AXES + z) * AXES + y for x in range(AXES) for y in range(AXES)] for z in range(AXES)
    ]


def z_pairs(step):
    return [(i, i ^ (step * AXES)) for i in range(AXES**3)]


def scattered(value):
    return lax.all_to_all(value, "space", 0, 0, axis_index_groups=groups_over_xy()).sum(axis=0)


def spread_kernel(a, b, c, d, out):
    total = (a[...] + b[...]) + (c[...] + d[...])
    for i in range(out.shape[0]):
        out[i] = total


def gathered(value):
    parts = [value] + [lax.ppermute(value, "space", z_pairs(step)) for step in (1, 2, 3)]
    pieces = pl.pallas_call(
        spread_kernel,
        out_shape=jax.ShapeDtypeStruct((AXES * AXES,) + value.shape, F32),
        in_specs=[pl.BlockSpec(memory_space=pltpu.VMEM)] * 4,
        out_specs=pl.BlockSpec(memory_space=pltpu.VMEM),
        compiler_params=pltpu.CompilerParams(vmem_limit_bytes=2 * 1024 * 1024),
        cost_estimate=pl.CostEstimate(flops=2**16, bytes_accessed=2**19, transcendentals=0),
        name="spread_kernel",
    )(*parts)
    return lax.all_to_all(pieces, "space", 0, 0, axis_index_groups=groups_over_xy())


def swap_halo(first, last):
    count = lax.axis_size("space")
    odd = lax.axis_index("space") % 2 == 1
    inner = [(i, i ^ 1) for i in range(count)]
    outer = [(i, i + 1) for i in range(1, count - 1, 2)]
    outer = outer + [(j, i) for i, j in outer]
    a = lax.ppermute(jnp.where(odd, first, last), "space", inner)
    b = lax.ppermute(jnp.where(odd, last, first), "space", outer)
    return a, b, odd


def per_device(inputs, out_grad, weights):
    channels, planes, rows, cols = inputs.shape
    filters = weights.shape[4]
    cell_total = planes * rows * lax.axis_size("space") * cols
    scale = 1.0 / math.sqrt(cell_total)
    x = inputs.reshape(-1, cols)
    g0 = out_grad.reshape(-1, cols)
    w = weights.reshape(-1, filters)
    across = [(i, i ^ 2) for i in range(4)]
    beside = [(i, i ^ 1) for i in range(4)]
    g2 = lax.ppermute(g0, "chan", across)
    g1 = lax.ppermute(g0, "chan", beside)
    near, far, odd = swap_halo(
        inputs[:, :, 0, :].reshape(-1, cols), inputs[:, :, 1, :].reshape(-1, cols)
    )
    g1, g2, near, far = lax.optimization_barrier((g1, g2, near, far))
    g3 = lax.ppermute(g2, "chan", beside)
    cells = planes * rows * cols

    def vmem(n):
        return [pl.BlockSpec(memory_space=pltpu.VMEM)] * n

    partial = pl.pallas_call(
        lambda *refs: weight_kernel(scale, planes, *refs),
        out_shape=jax.ShapeDtypeStruct((27 * channels, filters), F32),
        in_specs=vmem(7),
        out_specs=vmem(1)[0],
        scratch_shapes=[
            pltpu.VMEM((6 * channels, (planes + 2) * 4 * cols), BF),
            pltpu.VMEM((2 * filters, cells), BF),
        ],
        compiler_params=pltpu.CompilerParams(vmem_limit_bytes=48 * 1024 * 1024),
        cost_estimate=pl.CostEstimate(
            flops=6 * 27 * channels * filters * cells, bytes_accessed=2**21, transcendentals=0
        ),
        name="weight_kernel",
    )(x, near, far, g0, g1, g2, g3)
    partial, w, g0, g1, g2, g3 = lax.optimization_barrier((partial, w, g0, g1, g2, g3))
    piece = scattered(partial.reshape(AXES * AXES, -1, 2, filters))
    halo = jax.ShapeDtypeStruct((channels * planes, cols), F32)
    core, to_above, to_below = pl.pallas_call(
        lambda *refs: input_kernel(planes, *refs),
        out_shape=(jax.ShapeDtypeStruct(x.shape, F32), halo, halo),
        in_specs=vmem(5),
        out_specs=tuple(vmem(3)),
        scratch_shapes=[
            pltpu.VMEM((9 * channels, 9 * filters), BF),
            pltpu.VMEM((2 * filters, cells), BF),
        ],
        compiler_params=pltpu.CompilerParams(vmem_limit_bytes=48 * 1024 * 1024),
        cost_estimate=pl.CostEstimate(
            flops=6 * 27 * channels * filters * cells, bytes_accessed=2**21, transcendentals=0
        ),
        name="input_kernel",
    )(w, g0, g1, g2, g3)
    near, far, odd = swap_halo(to_above, to_below)
    weight_grad = gathered(piece)
    near = near.reshape(channels, planes, cols)
    far = far.reshape(channels, planes, cols)
    rims = jnp.stack([jnp.where(odd, near, far), jnp.where(odd, far, near)], axis=2)
    input_grad = core.reshape(inputs.shape) + rims
    weight_grad = weight_grad.reshape(3, 3, 3, channels, filters)
    return (input_grad, weight_grad)


def solution(mesh):
    return jax.shard_map(
        per_device,
        mesh=mesh,
        in_specs=(
            P("chan", None, "space", None),
            P("chan", None, "space", None),
            P(None, None, None, "chan", None),
        ),
        out_specs=(P("chan", None, "space", None), P(None, None, None, "chan", None)),
        check_vma=False,
    )
```

```python
import math

import jax
import jax.numpy as jnp
from jax import lax
from jax.experimental import pallas as pl
from jax.experimental.pallas import tpu as pltpu
from jax.sharding import PartitionSpec as P

BF = jnp.bfloat16
F32 = jnp.float32


def split(value):
    high = value.astype(BF)
    return high, (value - high.astype(F32)).astype(BF)


def shifted(value, step):
    lanes = value.shape[1]
    lane = lax.broadcasted_iota(jnp.int32, value.shape, 1)
    edge = lanes - 1 if step > 0 else 0
    return jnp.where(lane == edge, 0.0, pltpu.roll(value, (-step) % lanes, 1))


def load_grads(parts, grads, chan):
    filters = grads.shape[0] // 2
    count = filters // len(parts)
    pairs = parts[0].shape[0] // count
    for j, part in enumerate(parts):
        start = pl.multiple_of((chan ^ j) * count, count)
        for r in range(pairs):
            high, low = split(part[pl.ds(r, count, stride=pairs), :])
            grads[pl.ds(start, count), r * 128 : (r + 1) * 128] = high
            grads[pl.ds(filters + start, count), r * 128 : (r + 1) * 128] = low


def weight_kernel(scale, planes, x, near, far, g0, g1, g2, g3, out, cells, grads):
    chan = lax.axis_index("chan")
    load_grads((g0, g1, g2, g3), grads, chan)
    count = x.shape[0] // (2 * planes)
    filters = grads.shape[0] // 2
    cells[:, : 4 * 128] = jnp.zeros((cells.shape[0], 4 * 128), BF)
    cells[:, (planes + 1) * 512 :] = jnp.zeros((cells.shape[0], 512), BF)
    odd = lax.axis_index("space") % 2 == 1
    for d in range(planes):
        for r in range(4):
            if r in (0, 3):
                inner = near[pl.ds(d, count, stride=planes), :]
                outer = far[pl.ds(d, count, stride=planes), :]
                value = jnp.where(odd, inner, outer) if r == 0 else jnp.where(odd, outer, inner)
            else:
                value = x[pl.ds(2 * d + r - 1, count, stride=2 * planes), :]
            at = ((d + 1) * 4 + r) * 128
            for kw in range(3):
                moved = value if kw == 1 else shifted(value, kw - 1)
                high, low = split(moved)
                cells[kw * 2 * count : (kw * 2 + 1) * count, at : at + 128] = high
                cells[(kw * 2 + 1) * count : (kw * 2 + 2) * count, at : at + 128] = low
    for kh in range(3):
        stripes = []
        for kd in range(3):
            starts = [((d + kd) * 4 + kh) * 128 for d in range(planes)]
            stripes.append(jnp.concatenate([cells[:, i : i + 256] for i in starts], axis=1))
        full = lax.dot_general(
            jnp.concatenate(stripes, axis=0),
            grads[...],
            (((1,), (1,)), ((), ())),
            preferred_element_type=F32,
        )
        for kd in range(3):
            for kw in range(3):
                at = (kd * 3 + kw) * 2 * count
                high = full[at : at + count]
                low = full[at + count : at + 2 * count]
                total = high[:, :filters] + (high[:, filters:] + low[:, :filters])
                tap = (kd * 3 + kh) * 3 + kw
                out[tap * count : (tap + 1) * count, :] = total * scale


def input_kernel(planes, w, g0, g1, g2, g3, out, above, below, left, grads):
    chan = lax.axis_index("chan")
    load_grads((g0, g1, g2, g3), grads, chan)
    count = w.shape[0] // 27
    filters = grads.shape[0] // 2
    block = 9 * count
    for kd in range(3):
        high, low = split(w[kd * block : (kd + 1) * block, :])
        left[:, (kd * 3) * filters : (kd * 3 + 1) * filters] = high
        left[:, (kd * 3 + 1) * filters : (kd * 3 + 2) * filters] = low
        left[:, (kd * 3 + 2) * filters : (kd * 3 + 3) * filters] = high
    for q in range(planes):
        taps = [kd for kd in range(3) if 0 <= q - kd + 1 < planes]
        right = []
        for kd in taps:
            d = q - kd + 1
            high = grads[:filters, d * 256 : (d + 1) * 256]
            right += [high, high, grads[filters:, d * 256 : (d + 1) * 256]]
        full = jnp.dot(
            left[:, taps[0] * 3 * filters : (taps[-1] + 1) * 3 * filters],
            jnp.concatenate(right, axis=0),
            preferred_element_type=F32,
        )

        def term(kh, kw, h):
            at = (kh * 3 + kw) * count
            return full[at : at + count, h * 128 : (h + 1) * 128]

        def row(pairs):
            sums = []
            for kw in range(3):
                values = [term(kh, kw, h) for kh, h in pairs]
                sums.append(sum(values[1:], values[0]))
            return shifted(sums[0], 1) + sums[1] + shifted(sums[2], -1)

        out[pl.ds(2 * q, count, stride=2 * planes), :] = row([(1, 0), (0, 1)])
        out[pl.ds(2 * q + 1, count, stride=2 * planes), :] = row([(2, 0), (1, 1)])
        above[pl.ds(q, count, stride=planes), :] = row([(0, 0)])
        below[pl.ds(q, count, stride=planes), :] = row([(2, 1)])


AXES = 4


def groups_over_xy():
    return [
        [(x * AXES + z) * AXES + y for x in range(AXES) for y in range(AXES)] for z in range(AXES)
    ]


def z_pairs(step):
    return [(i, i ^ (step * AXES)) for i in range(AXES**3)]


def scattered(value):
    return lax.all_to_all(value, "space", 0, 0, axis_index_groups=groups_over_xy()).sum(axis=0)


def spread_kernel(a, b, c, d, out):
    total = (a[...] + b[...]) + (c[...] + d[...])
    for i in range(out.shape[0]):
        out[i] = total


def gathered(value):
    parts = [value] + [lax.ppermute(value, "space", z_pairs(step)) for step in (1, 3, 2)]
    pieces = pl.pallas_call(
        spread_kernel,
        out_shape=jax.ShapeDtypeStruct((AXES * AXES,) + value.shape, F32),
        in_specs=[pl.BlockSpec(memory_space=pltpu.VMEM)] * 4,
        out_specs=pl.BlockSpec(memory_space=pltpu.VMEM),
        compiler_params=pltpu.CompilerParams(vmem_limit_bytes=2 * 1024 * 1024),
        cost_estimate=pl.CostEstimate(flops=2**16, bytes_accessed=2**19, transcendentals=0),
        name="spread_kernel",
    )(*parts)
    return lax.all_to_all(pieces, "space", 0, 0, axis_index_groups=groups_over_xy())


def swap_halo(first, last):
    count = lax.axis_size("space")
    odd = lax.axis_index("space") % 2 == 1
    inner = [(i, i ^ 1) for i in range(count)]
    outer = [(i, i + 1) for i in range(1, count - 1, 2)]
    outer = outer + [(j, i) for i, j in outer]
    a = lax.ppermute(jnp.where(odd, first, last), "space", inner)
    b = lax.ppermute(jnp.where(odd, last, first), "space", outer)
    return a, b, odd


def per_device(inputs, out_grad, weights):
    channels, planes, rows, cols = inputs.shape
    filters = weights.shape[4]
    cell_total = planes * rows * lax.axis_size("space") * cols
    scale = 1.0 / math.sqrt(cell_total)
    x = inputs.reshape(-1, cols)
    g0 = out_grad.reshape(-1, cols)
    w = weights.reshape(-1, filters)
    across = [(i, i ^ 2) for i in range(4)]
    beside = [(i, i ^ 1) for i in range(4)]
    g2 = lax.ppermute(g0, "chan", across)
    g1 = lax.ppermute(g0, "chan", beside)
    near, far, odd = swap_halo(
        inputs[:, :, 0, :].reshape(-1, cols), inputs[:, :, 1, :].reshape(-1, cols)
    )
    g1, g2, near, far = lax.optimization_barrier((g1, g2, near, far))
    g3 = lax.ppermute(g2, "chan", beside)
    cells = planes * rows * cols

    def vmem(n):
        return [pl.BlockSpec(memory_space=pltpu.VMEM)] * n

    partial = pl.pallas_call(
        lambda *refs: weight_kernel(scale, planes, *refs),
        out_shape=jax.ShapeDtypeStruct((27 * channels, filters), F32),
        in_specs=vmem(7),
        out_specs=vmem(1)[0],
        scratch_shapes=[
            pltpu.VMEM((6 * channels, (planes + 2) * 4 * cols), BF),
            pltpu.VMEM((2 * filters, cells), BF),
        ],
        compiler_params=pltpu.CompilerParams(vmem_limit_bytes=48 * 1024 * 1024),
        cost_estimate=pl.CostEstimate(
            flops=6 * 27 * channels * filters * cells, bytes_accessed=2**21, transcendentals=0
        ),
        name="weight_kernel",
    )(x, near, far, g0, g1, g2, g3)
    partial, w, g0, g1, g2, g3 = lax.optimization_barrier((partial, w, g0, g1, g2, g3))
    piece = scattered(partial.reshape(AXES * AXES, -1, 2, filters))
    halo = jax.ShapeDtypeStruct((channels * planes, cols), F32)
    core, to_above, to_below = pl.pallas_call(
        lambda *refs: input_kernel(planes, *refs),
        out_shape=(jax.ShapeDtypeStruct(x.shape, F32), halo, halo),
        in_specs=vmem(5),
        out_specs=tuple(vmem(3)),
        scratch_shapes=[
            pltpu.VMEM((9 * channels, 9 * filters), BF),
            pltpu.VMEM((2 * filters, cells), BF),
        ],
        compiler_params=pltpu.CompilerParams(vmem_limit_bytes=48 * 1024 * 1024),
        cost_estimate=pl.CostEstimate(
            flops=6 * 27 * channels * filters * cells, bytes_accessed=2**21, transcendentals=0
        ),
        name="input_kernel",
    )(w, g0, g1, g2, g3)
    near, far, odd = swap_halo(to_above, to_below)
    weight_grad = gathered(piece)
    near = near.reshape(channels, planes, cols)
    far = far.reshape(channels, planes, cols)
    rims = jnp.stack([jnp.where(odd, near, far), jnp.where(odd, far, near)], axis=2)
    input_grad = core.reshape(inputs.shape) + rims
    weight_grad = weight_grad.reshape(3, 3, 3, channels, filters)
    return (input_grad, weight_grad)


def solution(mesh):
    return jax.shard_map(
        per_device,
        mesh=mesh,
        in_specs=(
            P("chan", None, "space", None),
            P("chan", None, "space", None),
            P(None, None, None, "chan", None),
        ),
        out_specs=(P("chan", None, "space", None), P(None, None, None, "chan", None)),
        check_vma=False,
    )
```

```python
import math

import jax
import jax.numpy as jnp
from jax import lax
from jax.experimental import pallas as pl
from jax.experimental.pallas import tpu as pltpu
from jax.sharding import PartitionSpec as P

BF = jnp.bfloat16
F32 = jnp.float32


def split(value):
    high = value.astype(BF)
    return high, (value - high.astype(F32)).astype(BF)


def shifted(value, step):
    lanes = value.shape[1]
    lane = lax.broadcasted_iota(jnp.int32, value.shape, 1)
    edge = lanes - 1 if step > 0 else 0
    return jnp.where(lane == edge, 0.0, pltpu.roll(value, (-step) % lanes, 1))


def load_grads(parts, grads, chan):
    filters = grads.shape[0] // 2
    count = filters // len(parts)
    pairs = parts[0].shape[0] // count
    for j, part in enumerate(parts):
        start = pl.multiple_of((chan ^ j) * count, count)
        for r in range(pairs):
            high, low = split(part[pl.ds(r, count, stride=pairs), :])
            grads[pl.ds(start, count), r * 128 : (r + 1) * 128] = high
            grads[pl.ds(filters + start, count), r * 128 : (r + 1) * 128] = low


def weight_kernel(scale, planes, x, near, far, g0, g1, g2, g3, out, cells, grads):
    chan = lax.axis_index("chan")
    load_grads((g0, g1, g2, g3), grads, chan)
    count = x.shape[0] // (2 * planes)
    filters = grads.shape[0] // 2
    cells[:, : 4 * 128] = jnp.zeros((cells.shape[0], 4 * 128), BF)
    cells[:, (planes + 1) * 512 :] = jnp.zeros((cells.shape[0], 512), BF)
    odd = lax.axis_index("space") % 2 == 1
    for d in range(planes):
        for r in range(4):
            if r in (0, 3):
                inner = near[pl.ds(d, count, stride=planes), :]
                outer = far[pl.ds(d, count, stride=planes), :]
                value = jnp.where(odd, inner, outer) if r == 0 else jnp.where(odd, outer, inner)
            else:
                value = x[pl.ds(2 * d + r - 1, count, stride=2 * planes), :]
            at = ((d + 1) * 4 + r) * 128
            for kw in range(3):
                moved = value if kw == 1 else shifted(value, kw - 1)
                high, low = split(moved)
                cells[kw * 2 * count : (kw * 2 + 1) * count, at : at + 128] = high
                cells[(kw * 2 + 1) * count : (kw * 2 + 2) * count, at : at + 128] = low
    for kh in range(3):
        stripes = []
        for kd in range(3):
            starts = [((d + kd) * 4 + kh) * 128 for d in range(planes)]
            stripes.append(jnp.concatenate([cells[:, i : i + 256] for i in starts], axis=1))
        full = lax.dot_general(
            jnp.concatenate(stripes, axis=0),
            grads[...],
            (((1,), (1,)), ((), ())),
            preferred_element_type=F32,
        )
        for kd in range(3):
            for kw in range(3):
                at = (kd * 3 + kw) * 2 * count
                high = full[at : at + count]
                low = full[at + count : at + 2 * count]
                total = high[:, :filters] + (high[:, filters:] + low[:, :filters])
                tap = (kd * 3 + kh) * 3 + kw
                out[tap * count : (tap + 1) * count, :] = total * scale


def input_kernel(planes, w, g0, g1, g2, g3, out, above, below, left, grads):
    chan = lax.axis_index("chan")
    load_grads((g0, g1, g2, g3), grads, chan)
    count = w.shape[0] // 27
    filters = grads.shape[0] // 2
    block = 9 * count
    for kd in range(3):
        high, low = split(w[kd * block : (kd + 1) * block, :])
        left[:, (kd * 3) * filters : (kd * 3 + 1) * filters] = high
        left[:, (kd * 3 + 1) * filters : (kd * 3 + 2) * filters] = low
        left[:, (kd * 3 + 2) * filters : (kd * 3 + 3) * filters] = high
    for q in range(planes):
        taps = [kd for kd in range(3) if 0 <= q - kd + 1 < planes]
        right = []
        for kd in taps:
            d = q - kd + 1
            high = grads[:filters, d * 256 : (d + 1) * 256]
            right += [high, high, grads[filters:, d * 256 : (d + 1) * 256]]
        full = jnp.dot(
            left[:, taps[0] * 3 * filters : (taps[-1] + 1) * 3 * filters],
            jnp.concatenate(right, axis=0),
            preferred_element_type=F32,
        )

        def term(kh, kw, h):
            at = (kh * 3 + kw) * count
            return full[at : at + count, h * 128 : (h + 1) * 128]

        def row(pairs):
            sums = []
            for kw in range(3):
                values = [term(kh, kw, h) for kh, h in pairs]
                sums.append(sum(values[1:], values[0]))
            return shifted(sums[0], 1) + sums[1] + shifted(sums[2], -1)

        out[pl.ds(2 * q, count, stride=2 * planes), :] = row([(1, 0), (0, 1)])
        out[pl.ds(2 * q + 1, count, stride=2 * planes), :] = row([(2, 0), (1, 1)])
        above[pl.ds(q, count, stride=planes), :] = row([(0, 0)])
        below[pl.ds(q, count, stride=planes), :] = row([(2, 1)])


AXES = 4


def groups_over_xy():
    return [
        [(x * AXES + z) * AXES + y for x in range(AXES) for y in range(AXES)] for z in range(AXES)
    ]


def z_pairs(step):
    return [(i, i ^ (step * AXES)) for i in range(AXES**3)]


def scattered(value):
    return lax.all_to_all(value, "space", 0, 0, axis_index_groups=groups_over_xy()).sum(axis=0)


def spread_kernel(a, b, c, d, out):
    total = (a[...] + b[...]) + (c[...] + d[...])
    for i in range(out.shape[0]):
        out[i] = total


def gathered(value):
    parts = [value] + [lax.ppermute(value, "space", z_pairs(step)) for step in (1, 3, 2)]
    pieces = pl.pallas_call(
        spread_kernel,
        out_shape=jax.ShapeDtypeStruct((AXES * AXES,) + value.shape, F32),
        in_specs=[pl.BlockSpec(memory_space=pltpu.VMEM)] * 4,
        out_specs=pl.BlockSpec(memory_space=pltpu.VMEM),
        compiler_params=pltpu.CompilerParams(vmem_limit_bytes=2 * 1024 * 1024),
        cost_estimate=pl.CostEstimate(flops=2**16, bytes_accessed=2**19, transcendentals=0),
        name="spread_kernel",
    )(*parts)
    return lax.all_to_all(pieces, "space", 0, 0, axis_index_groups=groups_over_xy())


def swap_halo(first, last):
    count = lax.axis_size("space")
    odd = lax.axis_index("space") % 2 == 1
    inner = [(i, i ^ 1) for i in range(count)]
    outer = [(i, i + 1) for i in range(1, count - 1, 2)]
    outer = outer + [(j, i) for i, j in outer]
    a = lax.ppermute(jnp.where(odd, first, last), "space", inner)
    b = lax.ppermute(jnp.where(odd, last, first), "space", outer)
    return a, b, odd


def keep_kernel(value, out):
    out[...] = value[...]


def per_device(inputs, out_grad, weights):
    channels, planes, rows, cols = inputs.shape
    filters = weights.shape[4]
    cell_total = planes * rows * lax.axis_size("space") * cols
    scale = 1.0 / math.sqrt(cell_total)
    x = inputs.reshape(-1, cols)
    g0 = out_grad.reshape(-1, cols)
    w = weights.reshape(-1, filters)
    across = [(i, i ^ 2) for i in range(4)]
    beside = [(i, i ^ 1) for i in range(4)]
    g2 = lax.ppermute(g0, "chan", across)
    g1 = lax.ppermute(g0, "chan", beside)
    near, far, odd = swap_halo(
        inputs[:, :, 0, :].reshape(-1, cols), inputs[:, :, 1, :].reshape(-1, cols)
    )
    g1, g2, near = lax.optimization_barrier((g1, g2, near))
    g3 = lax.ppermute(g2, "chan", beside)
    far = pl.pallas_call(
        keep_kernel,
        out_shape=jax.ShapeDtypeStruct(far.shape, F32),
        in_specs=[pl.BlockSpec(memory_space=pltpu.VMEM)],
        out_specs=pl.BlockSpec(memory_space=pltpu.VMEM),
        compiler_params=pltpu.CompilerParams(vmem_limit_bytes=2 * 1024 * 1024),
        cost_estimate=pl.CostEstimate(flops=3 * 10**9, bytes_accessed=2**18, transcendentals=0),
        name="keep_kernel",
    )(far)
    cells = planes * rows * cols

    def vmem(n):
        return [pl.BlockSpec(memory_space=pltpu.VMEM)] * n

    partial = pl.pallas_call(
        lambda *refs: weight_kernel(scale, planes, *refs),
        out_shape=jax.ShapeDtypeStruct((27 * channels, filters), F32),
        in_specs=vmem(7),
        out_specs=vmem(1)[0],
        scratch_shapes=[
            pltpu.VMEM((6 * channels, (planes + 2) * 4 * cols), BF),
            pltpu.VMEM((2 * filters, cells), BF),
        ],
        compiler_params=pltpu.CompilerParams(vmem_limit_bytes=48 * 1024 * 1024),
        cost_estimate=pl.CostEstimate(
            flops=6 * 27 * channels * filters * cells, bytes_accessed=2**21, transcendentals=0
        ),
        name="weight_kernel",
    )(x, near, far, g0, g1, g2, g3)
    partial, w, g0, g1, g2, g3 = lax.optimization_barrier((partial, w, g0, g1, g2, g3))
    piece = scattered(partial.reshape(AXES * AXES, -1, 2, filters))
    halo = jax.ShapeDtypeStruct((channels * planes, cols), F32)
    core, to_above, to_below = pl.pallas_call(
        lambda *refs: input_kernel(planes, *refs),
        out_shape=(jax.ShapeDtypeStruct(x.shape, F32), halo, halo),
        in_specs=vmem(5),
        out_specs=tuple(vmem(3)),
        scratch_shapes=[
            pltpu.VMEM((9 * channels, 9 * filters), BF),
            pltpu.VMEM((2 * filters, cells), BF),
        ],
        compiler_params=pltpu.CompilerParams(vmem_limit_bytes=48 * 1024 * 1024),
        cost_estimate=pl.CostEstimate(
            flops=6 * 27 * channels * filters * cells, bytes_accessed=2**21, transcendentals=0
        ),
        name="input_kernel",
    )(w, g0, g1, g2, g3)
    near, far, odd = swap_halo(to_above, to_below)
    weight_grad = gathered(piece)
    near = near.reshape(channels, planes, cols)
    far = far.reshape(channels, planes, cols)
    rims = jnp.stack([jnp.where(odd, near, far), jnp.where(odd, far, near)], axis=2)
    input_grad = core.reshape(inputs.shape) + rims
    weight_grad = weight_grad.reshape(3, 3, 3, channels, filters)
    return (input_grad, weight_grad)


def solution(mesh):
    return jax.shard_map(
        per_device,
        mesh=mesh,
        in_specs=(
            P("chan", None, "space", None),
            P("chan", None, "space", None),
            P(None, None, None, "chan", None),
        ),
        out_specs=(P("chan", None, "space", None), P(None, None, None, "chan", None)),
        check_vma=False,
    )
```

```python
import math

import jax
import jax.numpy as jnp
from jax import lax
from jax.experimental import pallas as pl
from jax.experimental.pallas import tpu as pltpu
from jax.sharding import PartitionSpec as P

BF = jnp.bfloat16
F32 = jnp.float32


def split(value):
    high = value.astype(BF)
    return high, (value - high.astype(F32)).astype(BF)


def shifted(value, step):
    lanes = value.shape[1]
    lane = lax.broadcasted_iota(jnp.int32, value.shape, 1)
    edge = lanes - 1 if step > 0 else 0
    return jnp.where(lane == edge, 0.0, pltpu.roll(value, (-step) % lanes, 1))


def load_grads(parts, grads, chan):
    filters = grads.shape[0] // 2
    count = filters // len(parts)
    pairs = parts[0].shape[0] // count
    for j, part in enumerate(parts):
        start = pl.multiple_of((chan ^ j) * count, count)
        for r in range(pairs):
            high, low = split(part[pl.ds(r, count, stride=pairs), :])
            grads[pl.ds(start, count), r * 128 : (r + 1) * 128] = high
            grads[pl.ds(filters + start, count), r * 128 : (r + 1) * 128] = low


def weight_kernel(scale, planes, x, near, far, g0, g1, g2, g3, out, cells, grads):
    chan = lax.axis_index("chan")
    load_grads((g0, g1, g2, g3), grads, chan)
    count = x.shape[0] // (2 * planes)
    filters = grads.shape[0] // 2
    cells[:, : 4 * 128] = jnp.zeros((cells.shape[0], 4 * 128), BF)
    cells[:, (planes + 1) * 512 :] = jnp.zeros((cells.shape[0], 512), BF)
    odd = lax.axis_index("space") % 2 == 1
    for d in range(planes):
        for r in range(4):
            if r in (0, 3):
                inner = near[pl.ds(d, count, stride=planes), :]
                outer = far[pl.ds(d, count, stride=planes), :]
                value = jnp.where(odd, inner, outer) if r == 0 else jnp.where(odd, outer, inner)
            else:
                value = x[pl.ds(2 * d + r - 1, count, stride=2 * planes), :]
            at = ((d + 1) * 4 + r) * 128
            for kw in range(3):
                moved = value if kw == 1 else shifted(value, kw - 1)
                high, low = split(moved)
                cells[kw * 2 * count : (kw * 2 + 1) * count, at : at + 128] = high
                cells[(kw * 2 + 1) * count : (kw * 2 + 2) * count, at : at + 128] = low
    for kh in range(3):
        stripes = []
        for kd in range(3):
            starts = [((d + kd) * 4 + kh) * 128 for d in range(planes)]
            stripes.append(jnp.concatenate([cells[:, i : i + 256] for i in starts], axis=1))
        full = lax.dot_general(
            jnp.concatenate(stripes, axis=0),
            grads[...],
            (((1,), (1,)), ((), ())),
            preferred_element_type=F32,
        )
        for kd in range(3):
            for kw in range(3):
                at = (kd * 3 + kw) * 2 * count
                high = full[at : at + count]
                low = full[at + count : at + 2 * count]
                total = high[:, :filters] + (high[:, filters:] + low[:, :filters])
                tap = (kd * 3 + kh) * 3 + kw
                out[tap * count : (tap + 1) * count, :] = total * scale


def input_kernel(planes, w, g0, g1, g2, g3, out, above, below, left, grads):
    chan = lax.axis_index("chan")
    load_grads((g0, g1, g2, g3), grads, chan)
    count = w.shape[0] // 27
    filters = grads.shape[0] // 2
    block = 9 * count
    for kd in range(3):
        high, low = split(w[kd * block : (kd + 1) * block, :])
        left[:, (kd * 3) * filters : (kd * 3 + 1) * filters] = high
        left[:, (kd * 3 + 1) * filters : (kd * 3 + 2) * filters] = low
        left[:, (kd * 3 + 2) * filters : (kd * 3 + 3) * filters] = high
    for q in range(planes):
        taps = [kd for kd in range(3) if 0 <= q - kd + 1 < planes]
        right = []
        for kd in taps:
            d = q - kd + 1
            high = grads[:filters, d * 256 : (d + 1) * 256]
            right += [high, high, grads[filters:, d * 256 : (d + 1) * 256]]
        full = jnp.dot(
            left[:, taps[0] * 3 * filters : (taps[-1] + 1) * 3 * filters],
            jnp.concatenate(right, axis=0),
            preferred_element_type=F32,
        )

        def term(kh, kw, h):
            at = (kh * 3 + kw) * count
            return full[at : at + count, h * 128 : (h + 1) * 128]

        def row(pairs):
            sums = []
            for kw in range(3):
                values = [term(kh, kw, h) for kh, h in pairs]
                sums.append(sum(values[1:], values[0]))
            return shifted(sums[0], 1) + sums[1] + shifted(sums[2], -1)

        out[pl.ds(2 * q, count, stride=2 * planes), :] = row([(1, 0), (0, 1)])
        out[pl.ds(2 * q + 1, count, stride=2 * planes), :] = row([(2, 0), (1, 1)])
        above[pl.ds(q, count, stride=planes), :] = row([(0, 0)])
        below[pl.ds(q, count, stride=planes), :] = row([(2, 1)])


AXES = 4


def groups_over_xy():
    return [
        [(x * AXES + z) * AXES + y for x in range(AXES) for y in range(AXES)] for z in range(AXES)
    ]


def z_pairs(step):
    return [(i, i ^ (step * AXES)) for i in range(AXES**3)]


def scattered(value):
    return lax.all_to_all(value, "space", 0, 0, axis_index_groups=groups_over_xy()).sum(axis=0)


def spread_kernel(a, b, c, d, out):
    total = (a[...] + b[...]) + (c[...] + d[...])
    for i in range(out.shape[0]):
        out[i] = total


def gathered(value):
    parts = [value] + [lax.ppermute(value, "space", z_pairs(step)) for step in (1, 2, 3)]
    pieces = pl.pallas_call(
        spread_kernel,
        out_shape=jax.ShapeDtypeStruct((AXES * AXES,) + value.shape, F32),
        in_specs=[pl.BlockSpec(memory_space=pltpu.VMEM)] * 4,
        out_specs=pl.BlockSpec(memory_space=pltpu.VMEM),
        compiler_params=pltpu.CompilerParams(vmem_limit_bytes=2 * 1024 * 1024),
        cost_estimate=pl.CostEstimate(flops=2**16, bytes_accessed=2**19, transcendentals=0),
        name="spread_kernel",
    )(*parts)
    return lax.all_to_all(pieces, "space", 0, 0, axis_index_groups=groups_over_xy())


def swap_halo(first, last):
    count = lax.axis_size("space")
    odd = lax.axis_index("space") % 2 == 1
    inner = [(i, i ^ 1) for i in range(count)]
    outer = [(i, i + 1) for i in range(1, count - 1, 2)]
    outer = outer + [(j, i) for i, j in outer]
    a = lax.ppermute(jnp.where(odd, first, last), "space", inner)
    b = lax.ppermute(jnp.where(odd, last, first), "space", outer)
    return a, b, odd


def keep_kernel(value, out):
    out[...] = value[...]


def per_device(inputs, out_grad, weights):
    channels, planes, rows, cols = inputs.shape
    filters = weights.shape[4]
    cell_total = planes * rows * lax.axis_size("space") * cols
    scale = 1.0 / math.sqrt(cell_total)
    x = inputs.reshape(-1, cols)
    g0 = out_grad.reshape(-1, cols)
    w = weights.reshape(-1, filters)
    across = [(i, i ^ 2) for i in range(4)]
    beside = [(i, i ^ 1) for i in range(4)]
    g2 = lax.ppermute(g0, "chan", across)
    g1 = lax.ppermute(g0, "chan", beside)
    near, far, odd = swap_halo(
        inputs[:, :, 0, :].reshape(-1, cols), inputs[:, :, 1, :].reshape(-1, cols)
    )
    g1, g2, near = lax.optimization_barrier((g1, g2, near))
    g3 = lax.ppermute(g2, "chan", beside)
    far = pl.pallas_call(
        keep_kernel,
        out_shape=jax.ShapeDtypeStruct(far.shape, F32),
        in_specs=[pl.BlockSpec(memory_space=pltpu.VMEM)],
        out_specs=pl.BlockSpec(memory_space=pltpu.VMEM),
        compiler_params=pltpu.CompilerParams(vmem_limit_bytes=2 * 1024 * 1024),
        cost_estimate=pl.CostEstimate(flops=3 * 10**9, bytes_accessed=2**18, transcendentals=0),
        name="keep_kernel",
    )(far)
    cells = planes * rows * cols

    def vmem(n):
        return [pl.BlockSpec(memory_space=pltpu.VMEM)] * n

    partial = pl.pallas_call(
        lambda *refs: weight_kernel(scale, planes, *refs),
        out_shape=jax.ShapeDtypeStruct((27 * channels, filters), F32),
        in_specs=vmem(7),
        out_specs=vmem(1)[0],
        scratch_shapes=[
            pltpu.VMEM((6 * channels, (planes + 2) * 4 * cols), BF),
            pltpu.VMEM((2 * filters, cells), BF),
        ],
        compiler_params=pltpu.CompilerParams(vmem_limit_bytes=48 * 1024 * 1024),
        cost_estimate=pl.CostEstimate(
            flops=6 * 27 * channels * filters * cells, bytes_accessed=2**21, transcendentals=0
        ),
        name="weight_kernel",
    )(x, near, far, g0, g1, g2, g3)
    partial, w, g0, g1, g2, g3 = lax.optimization_barrier((partial, w, g0, g1, g2, g3))
    piece = scattered(partial.reshape(AXES * AXES, -1, 2, filters))
    halo = jax.ShapeDtypeStruct((channels * planes, cols), F32)
    core, to_above, to_below = pl.pallas_call(
        lambda *refs: input_kernel(planes, *refs),
        out_shape=(jax.ShapeDtypeStruct(x.shape, F32), halo, halo),
        in_specs=vmem(5),
        out_specs=tuple(vmem(3)),
        scratch_shapes=[
            pltpu.VMEM((9 * channels, 9 * filters), BF),
            pltpu.VMEM((2 * filters, cells), BF),
        ],
        compiler_params=pltpu.CompilerParams(vmem_limit_bytes=48 * 1024 * 1024),
        cost_estimate=pl.CostEstimate(
            flops=6 * 27 * channels * filters * cells, bytes_accessed=2**21, transcendentals=0
        ),
        name="input_kernel",
    )(w, g0, g1, g2, g3)
    near, far, odd = swap_halo(to_above, to_below)
    weight_grad = gathered(piece)
    near = near.reshape(channels, planes, cols)
    far = far.reshape(channels, planes, cols)
    rims = jnp.stack([jnp.where(odd, near, far), jnp.where(odd, far, near)], axis=2)
    input_grad = core.reshape(inputs.shape) + rims
    weight_grad = weight_grad.reshape(3, 3, 3, channels, filters)
    return (input_grad, weight_grad)


def solution(mesh):
    return jax.shard_map(
        per_device,
        mesh=mesh,
        in_specs=(
            P("chan", None, "space", None),
            P("chan", None, "space", None),
            P(None, None, None, "chan", None),
        ),
        out_specs=(P("chan", None, "space", None), P(None, None, None, "chan", None)),
        check_vma=False,
    )
```

```python
import math

import jax
import jax.numpy as jnp
from jax import lax
from jax.experimental import pallas as pl
from jax.experimental.pallas import tpu as pltpu
from jax.sharding import PartitionSpec as P

BF = jnp.bfloat16
F32 = jnp.float32


def split(value):
    high = value.astype(BF)
    return high, (value - high.astype(F32)).astype(BF)


def shifted(value, step):
    lanes = value.shape[1]
    lane = lax.broadcasted_iota(jnp.int32, value.shape, 1)
    edge = lanes - 1 if step > 0 else 0
    return jnp.where(lane == edge, 0.0, pltpu.roll(value, (-step) % lanes, 1))


def load_grads(parts, grads, chan):
    filters = grads.shape[0] // 2
    count = filters // len(parts)
    pairs = parts[0].shape[0] // count
    for j, part in enumerate(parts):
        start = pl.multiple_of((chan ^ j) * count, count)
        for r in range(pairs):
            high, low = split(part[pl.ds(r, count, stride=pairs), :])
            grads[pl.ds(start, count), r * 128 : (r + 1) * 128] = high
            grads[pl.ds(filters + start, count), r * 128 : (r + 1) * 128] = low


def weight_kernel(scale, planes, x, near, far, g0, g1, g2, g3, out, cells, grads):
    chan = lax.axis_index("chan")
    load_grads((g0, g1, g2, g3), grads, chan)
    count = x.shape[0] // (2 * planes)
    filters = grads.shape[0] // 2
    cells[:, : 4 * 128] = jnp.zeros((cells.shape[0], 4 * 128), BF)
    cells[:, (planes + 1) * 512 :] = jnp.zeros((cells.shape[0], 512), BF)
    odd = lax.axis_index("space") % 2 == 1
    for d in range(planes):
        for r in range(4):
            if r in (0, 3):
                inner = near[pl.ds(d, count, stride=planes), :]
                outer = far[pl.ds(d, count, stride=planes), :]
                value = jnp.where(odd, inner, outer) if r == 0 else jnp.where(odd, outer, inner)
            else:
                value = x[pl.ds(2 * d + r - 1, count, stride=2 * planes), :]
            at = ((d + 1) * 4 + r) * 128
            for kw in range(3):
                moved = value if kw == 1 else shifted(value, kw - 1)
                high, low = split(moved)
                cells[kw * 2 * count : (kw * 2 + 1) * count, at : at + 128] = high
                cells[(kw * 2 + 1) * count : (kw * 2 + 2) * count, at : at + 128] = low
    for kh in range(3):
        stripes = []
        for kd in range(3):
            starts = [((d + kd) * 4 + kh) * 128 for d in range(planes)]
            stripes.append(jnp.concatenate([cells[:, i : i + 256] for i in starts], axis=1))
        full = lax.dot_general(
            jnp.concatenate(stripes, axis=0),
            grads[...],
            (((1,), (1,)), ((), ())),
            preferred_element_type=F32,
        )
        for kd in range(3):
            for kw in range(3):
                at = (kd * 3 + kw) * 2 * count
                high = full[at : at + count]
                low = full[at + count : at + 2 * count]
                total = high[:, :filters] + (high[:, filters:] + low[:, :filters])
                tap = (kd * 3 + kh) * 3 + kw
                out[tap * count : (tap + 1) * count, :] = total * scale


def input_kernel(planes, w, g0, g1, g2, g3, out, above, below, left, grads):
    chan = lax.axis_index("chan")
    load_grads((g0, g1, g2, g3), grads, chan)
    count = w.shape[0] // 27
    filters = grads.shape[0] // 2
    block = 9 * count
    for kd in range(3):
        high, low = split(w[kd * block : (kd + 1) * block, :])
        left[:, (kd * 3) * filters : (kd * 3 + 1) * filters] = high
        left[:, (kd * 3 + 1) * filters : (kd * 3 + 2) * filters] = low
        left[:, (kd * 3 + 2) * filters : (kd * 3 + 3) * filters] = high
    for q in range(planes):
        taps = [kd for kd in range(3) if 0 <= q - kd + 1 < planes]
        right = []
        for kd in taps:
            d = q - kd + 1
            high = grads[:filters, d * 256 : (d + 1) * 256]
            right += [high, high, grads[filters:, d * 256 : (d + 1) * 256]]
        full = jnp.dot(
            left[:, taps[0] * 3 * filters : (taps[-1] + 1) * 3 * filters],
            jnp.concatenate(right, axis=0),
            preferred_element_type=F32,
        )

        def term(kh, kw, h):
            at = (kh * 3 + kw) * count
            return full[at : at + count, h * 128 : (h + 1) * 128]

        def row(pairs):
            sums = []
            for kw in range(3):
                values = [term(kh, kw, h) for kh, h in pairs]
                sums.append(sum(values[1:], values[0]))
            return shifted(sums[0], 1) + sums[1] + shifted(sums[2], -1)

        out[pl.ds(2 * q, count, stride=2 * planes), :] = row([(1, 0), (0, 1)])
        out[pl.ds(2 * q + 1, count, stride=2 * planes), :] = row([(2, 0), (1, 1)])
        above[pl.ds(q, count, stride=planes), :] = row([(0, 0)])
        below[pl.ds(q, count, stride=planes), :] = row([(2, 1)])


AXES = 4


def groups_over_xy():
    return [
        [(x * AXES + z) * AXES + y for x in range(AXES) for y in range(AXES)] for z in range(AXES)
    ]


def z_pairs(step):
    return [(i, i ^ (step * AXES)) for i in range(AXES**3)]


def scattered(value):
    return lax.all_to_all(value, "space", 0, 0, axis_index_groups=groups_over_xy()).sum(axis=0)


def spread_kernel(a, b, c, d, out):
    total = (a[...] + b[...]) + (c[...] + d[...])
    for i in range(out.shape[0]):
        out[i] = total


def gathered(value):
    parts = [value] + [lax.ppermute(value, "space", z_pairs(step)) for step in (1, 2, 3)]
    pieces = pl.pallas_call(
        spread_kernel,
        out_shape=jax.ShapeDtypeStruct((AXES * AXES,) + value.shape, F32),
        in_specs=[pl.BlockSpec(memory_space=pltpu.VMEM)] * 4,
        out_specs=pl.BlockSpec(memory_space=pltpu.VMEM),
        compiler_params=pltpu.CompilerParams(vmem_limit_bytes=2 * 1024 * 1024),
        cost_estimate=pl.CostEstimate(flops=2**16, bytes_accessed=2**19, transcendentals=0),
        name="spread_kernel",
    )(*parts)
    return lax.all_to_all(pieces, "space", 0, 0, axis_index_groups=groups_over_xy())


def swap_halo(first, last):
    count = lax.axis_size("space")
    odd = lax.axis_index("space") % 2 == 1
    inner = [(i, i ^ 1) for i in range(count)]
    outer = [(i, i + 1) for i in range(1, count - 1, 2)]
    outer = outer + [(j, i) for i, j in outer]
    a = lax.ppermute(jnp.where(odd, first, last), "space", inner)
    b = lax.ppermute(jnp.where(odd, last, first), "space", outer)
    return a, b, odd


def keep_kernel(a, b, a_out, b_out):
    a_out[...] = a[...]
    b_out[...] = b[...]


def per_device(inputs, out_grad, weights):
    channels, planes, rows, cols = inputs.shape
    filters = weights.shape[4]
    cell_total = planes * rows * lax.axis_size("space") * cols
    scale = 1.0 / math.sqrt(cell_total)
    x = inputs.reshape(-1, cols)
    g0 = out_grad.reshape(-1, cols)
    w = weights.reshape(-1, filters)
    across = [(i, i ^ 2) for i in range(4)]
    beside = [(i, i ^ 1) for i in range(4)]
    g2 = lax.ppermute(g0, "chan", across)
    g1 = lax.ppermute(g0, "chan", beside)
    near, far, odd = swap_halo(
        inputs[:, :, 0, :].reshape(-1, cols), inputs[:, :, 1, :].reshape(-1, cols)
    )
    g1, g2 = lax.optimization_barrier((g1, g2))
    g3 = lax.ppermute(g2, "chan", beside)
    far, near = pl.pallas_call(
        keep_kernel,
        out_shape=(jax.ShapeDtypeStruct(far.shape, F32),) * 2,
        in_specs=[pl.BlockSpec(memory_space=pltpu.VMEM)] * 2,
        out_specs=(pl.BlockSpec(memory_space=pltpu.VMEM),) * 2,
        compiler_params=pltpu.CompilerParams(vmem_limit_bytes=2 * 1024 * 1024),
        cost_estimate=pl.CostEstimate(flops=3 * 10**9, bytes_accessed=2**18, transcendentals=0),
        name="keep_kernel",
    )(far, near)
    cells = planes * rows * cols

    def vmem(n):
        return [pl.BlockSpec(memory_space=pltpu.VMEM)] * n

    partial = pl.pallas_call(
        lambda *refs: weight_kernel(scale, planes, *refs),
        out_shape=jax.ShapeDtypeStruct((27 * channels, filters), F32),
        in_specs=vmem(7),
        out_specs=vmem(1)[0],
        scratch_shapes=[
            pltpu.VMEM((6 * channels, (planes + 2) * 4 * cols), BF),
            pltpu.VMEM((2 * filters, cells), BF),
        ],
        compiler_params=pltpu.CompilerParams(vmem_limit_bytes=48 * 1024 * 1024),
        cost_estimate=pl.CostEstimate(
            flops=6 * 27 * channels * filters * cells, bytes_accessed=2**21, transcendentals=0
        ),
        name="weight_kernel",
    )(x, near, far, g0, g1, g2, g3)
    partial, w, g0, g1, g2, g3 = lax.optimization_barrier((partial, w, g0, g1, g2, g3))
    piece = scattered(partial.reshape(AXES * AXES, -1, 2, filters))
    halo = jax.ShapeDtypeStruct((channels * planes, cols), F32)
    core, to_above, to_below = pl.pallas_call(
        lambda *refs: input_kernel(planes, *refs),
        out_shape=(jax.ShapeDtypeStruct(x.shape, F32), halo, halo),
        in_specs=vmem(5),
        out_specs=tuple(vmem(3)),
        scratch_shapes=[
            pltpu.VMEM((9 * channels, 9 * filters), BF),
            pltpu.VMEM((2 * filters, cells), BF),
        ],
        compiler_params=pltpu.CompilerParams(vmem_limit_bytes=48 * 1024 * 1024),
        cost_estimate=pl.CostEstimate(
            flops=6 * 27 * channels * filters * cells, bytes_accessed=2**21, transcendentals=0
        ),
        name="input_kernel",
    )(w, g0, g1, g2, g3)
    near, far, odd = swap_halo(to_above, to_below)
    weight_grad = gathered(piece)
    near = near.reshape(channels, planes, cols)
    far = far.reshape(channels, planes, cols)
    rims = jnp.stack([jnp.where(odd, near, far), jnp.where(odd, far, near)], axis=2)
    input_grad = core.reshape(inputs.shape) + rims
    weight_grad = weight_grad.reshape(3, 3, 3, channels, filters)
    return (input_grad, weight_grad)


def solution(mesh):
    return jax.shard_map(
        per_device,
        mesh=mesh,
        in_specs=(
            P("chan", None, "space", None),
            P("chan", None, "space", None),
            P(None, None, None, "chan", None),
        ),
        out_specs=(P("chan", None, "space", None), P(None, None, None, "chan", None)),
        check_vma=False,
    )
```

```python
import math

import jax
import jax.numpy as jnp
from jax import lax
from jax.experimental import pallas as pl
from jax.experimental.pallas import tpu as pltpu
from jax.sharding import PartitionSpec as P

BF = jnp.bfloat16
F32 = jnp.float32


def split(value):
    high = value.astype(BF)
    return high, (value - high.astype(F32)).astype(BF)


def shifted(value, step):
    lanes = value.shape[1]
    lane = lax.broadcasted_iota(jnp.int32, value.shape, 1)
    edge = lanes - 1 if step > 0 else 0
    return jnp.where(lane == edge, 0.0, pltpu.roll(value, (-step) % lanes, 1))


def load_grads(parts, grads, chan):
    filters = grads.shape[0] // 2
    count = filters // len(parts)
    pairs = parts[0].shape[0] // count
    for j, part in enumerate(parts):
        start = pl.multiple_of((chan ^ j) * count, count)
        for r in range(pairs):
            high, low = split(part[pl.ds(r, count, stride=pairs), :])
            grads[pl.ds(start, count), r * 128 : (r + 1) * 128] = high
            grads[pl.ds(filters + start, count), r * 128 : (r + 1) * 128] = low


def weight_kernel(scale, planes, x, near, far, g0, g1, g2, g3, out, cells, grads):
    chan = lax.axis_index("chan")
    load_grads((g0, g1, g2, g3), grads, chan)
    count = x.shape[0] // (2 * planes)
    filters = grads.shape[0] // 2
    cells[:, : 4 * 128] = jnp.zeros((cells.shape[0], 4 * 128), BF)
    cells[:, (planes + 1) * 512 :] = jnp.zeros((cells.shape[0], 512), BF)
    odd = lax.axis_index("space") % 2 == 1
    for d in range(planes):
        for r in range(4):
            if r in (0, 3):
                inner = near[pl.ds(d, count, stride=planes), :]
                outer = far[pl.ds(d, count, stride=planes), :]
                value = jnp.where(odd, inner, outer) if r == 0 else jnp.where(odd, outer, inner)
            else:
                value = x[pl.ds(2 * d + r - 1, count, stride=2 * planes), :]
            at = ((d + 1) * 4 + r) * 128
            for kw in range(3):
                moved = value if kw == 1 else shifted(value, kw - 1)
                high, low = split(moved)
                cells[kw * 2 * count : (kw * 2 + 1) * count, at : at + 128] = high
                cells[(kw * 2 + 1) * count : (kw * 2 + 2) * count, at : at + 128] = low
    for kh in range(3):
        stripes = []
        for kd in range(3):
            starts = [((d + kd) * 4 + kh) * 128 for d in range(planes)]
            stripes.append(jnp.concatenate([cells[:, i : i + 256] for i in starts], axis=1))
        full = lax.dot_general(
            jnp.concatenate(stripes, axis=0),
            grads[...],
            (((1,), (1,)), ((), ())),
            preferred_element_type=F32,
        )
        for kd in range(3):
            for kw in range(3):
                at = (kd * 3 + kw) * 2 * count
                high = full[at : at + count]
                low = full[at + count : at + 2 * count]
                total = high[:, :filters] + (high[:, filters:] + low[:, :filters])
                tap = (kd * 3 + kh) * 3 + kw
                out[tap * count : (tap + 1) * count, :] = total * scale


def input_kernel(planes, w, g0, g1, g2, g3, out, above, below, left, grads):
    chan = lax.axis_index("chan")
    load_grads((g0, g1, g2, g3), grads, chan)
    count = w.shape[0] // 27
    filters = grads.shape[0] // 2
    block = 9 * count
    for kd in range(3):
        high, low = split(w[kd * block : (kd + 1) * block, :])
        left[:, (kd * 3) * filters : (kd * 3 + 1) * filters] = high
        left[:, (kd * 3 + 1) * filters : (kd * 3 + 2) * filters] = low
        left[:, (kd * 3 + 2) * filters : (kd * 3 + 3) * filters] = high
    for q in range(planes):
        taps = [kd for kd in range(3) if 0 <= q - kd + 1 < planes]
        right = []
        for kd in taps:
            d = q - kd + 1
            high = grads[:filters, d * 256 : (d + 1) * 256]
            right += [high, high, grads[filters:, d * 256 : (d + 1) * 256]]
        full = jnp.dot(
            left[:, taps[0] * 3 * filters : (taps[-1] + 1) * 3 * filters],
            jnp.concatenate(right, axis=0),
            preferred_element_type=F32,
        )

        def term(kh, kw, h):
            at = (kh * 3 + kw) * count
            return full[at : at + count, h * 128 : (h + 1) * 128]

        def row(pairs):
            sums = []
            for kw in range(3):
                values = [term(kh, kw, h) for kh, h in pairs]
                sums.append(sum(values[1:], values[0]))
            return shifted(sums[0], 1) + sums[1] + shifted(sums[2], -1)

        out[pl.ds(2 * q, count, stride=2 * planes), :] = row([(1, 0), (0, 1)])
        out[pl.ds(2 * q + 1, count, stride=2 * planes), :] = row([(2, 0), (1, 1)])
        above[pl.ds(q, count, stride=planes), :] = row([(0, 0)])
        below[pl.ds(q, count, stride=planes), :] = row([(2, 1)])


AXES = 4


def groups_over_xy():
    return [
        [(x * AXES + z) * AXES + y for x in range(AXES) for y in range(AXES)] for z in range(AXES)
    ]


def z_pairs(step):
    return [(i, i ^ (step * AXES)) for i in range(AXES**3)]


def scattered(value):
    return lax.all_to_all(value, "space", 0, 0, axis_index_groups=groups_over_xy()).sum(axis=0)


def spread_kernel(a, b, c, d, out):
    total = (a[...] + b[...]) + (c[...] + d[...])
    for i in range(out.shape[0]):
        out[i] = total


def gathered(value):
    parts = [value] + [lax.ppermute(value, "space", z_pairs(step)) for step in (1, 2, 3)]
    pieces = pl.pallas_call(
        spread_kernel,
        out_shape=jax.ShapeDtypeStruct((AXES * AXES,) + value.shape, F32),
        in_specs=[pl.BlockSpec(memory_space=pltpu.VMEM)] * 4,
        out_specs=pl.BlockSpec(memory_space=pltpu.VMEM),
        compiler_params=pltpu.CompilerParams(vmem_limit_bytes=2 * 1024 * 1024),
        cost_estimate=pl.CostEstimate(flops=2**16, bytes_accessed=2**19, transcendentals=0),
        name="spread_kernel",
    )(*parts)
    return lax.all_to_all(pieces, "space", 0, 0, axis_index_groups=groups_over_xy())


def swap_halo(first, last):
    count = lax.axis_size("space")
    odd = lax.axis_index("space") % 2 == 1
    inner = [(i, i ^ 1) for i in range(count)]
    outer = [(i, i + 1) for i in range(1, count - 1, 2)]
    outer = outer + [(j, i) for i, j in outer]
    a = lax.ppermute(jnp.where(odd, first, last), "space", inner)
    b = lax.ppermute(jnp.where(odd, last, first), "space", outer)
    return a, b, odd


def keep_kernel(value, out):
    out[...] = value[...]


def per_device(inputs, out_grad, weights):
    channels, planes, rows, cols = inputs.shape
    filters = weights.shape[4]
    cell_total = planes * rows * lax.axis_size("space") * cols
    scale = 1.0 / math.sqrt(cell_total)
    x = inputs.reshape(-1, cols)
    g0 = out_grad.reshape(-1, cols)
    w = weights.reshape(-1, filters)
    across = [(i, i ^ 2) for i in range(4)]
    beside = [(i, i ^ 1) for i in range(4)]
    g2 = lax.ppermute(g0, "chan", across)
    g1 = lax.ppermute(g0, "chan", beside)
    near, far, odd = swap_halo(
        inputs[:, :, 0, :].reshape(-1, cols), inputs[:, :, 1, :].reshape(-1, cols)
    )
    g1, g2, near = lax.optimization_barrier((g1, g2, near))
    g3 = lax.ppermute(g2, "chan", beside)
    far = pl.pallas_call(
        keep_kernel,
        out_shape=jax.ShapeDtypeStruct(far.shape, F32),
        in_specs=[pl.BlockSpec(memory_space=pltpu.VMEM)],
        out_specs=pl.BlockSpec(memory_space=pltpu.VMEM),
        compiler_params=pltpu.CompilerParams(vmem_limit_bytes=2 * 1024 * 1024),
        cost_estimate=pl.CostEstimate(flops=3 * 10**9, bytes_accessed=2**18, transcendentals=0),
        name="keep_kernel",
    )(far)
    cells = planes * rows * cols

    def vmem(n):
        return [pl.BlockSpec(memory_space=pltpu.VMEM)] * n

    partial = pl.pallas_call(
        lambda *refs: weight_kernel(scale, planes, *refs),
        out_shape=jax.ShapeDtypeStruct((27 * channels, filters), F32),
        in_specs=vmem(7),
        out_specs=vmem(1)[0],
        scratch_shapes=[
            pltpu.VMEM((6 * channels, (planes + 2) * 4 * cols), BF),
            pltpu.VMEM((2 * filters, cells), BF),
        ],
        compiler_params=pltpu.CompilerParams(vmem_limit_bytes=16 * 1024 * 1024),
        cost_estimate=pl.CostEstimate(
            flops=6 * 27 * channels * filters * cells, bytes_accessed=2**21, transcendentals=0
        ),
        name="weight_kernel",
    )(x, near, far, g0, g1, g2, g3)
    partial, w, g0, g1, g2, g3 = lax.optimization_barrier((partial, w, g0, g1, g2, g3))
    piece = scattered(partial.reshape(AXES * AXES, -1, 2, filters))
    halo = jax.ShapeDtypeStruct((channels * planes, cols), F32)
    core, to_above, to_below = pl.pallas_call(
        lambda *refs: input_kernel(planes, *refs),
        out_shape=(jax.ShapeDtypeStruct(x.shape, F32), halo, halo),
        in_specs=vmem(5),
        out_specs=tuple(vmem(3)),
        scratch_shapes=[
            pltpu.VMEM((9 * channels, 9 * filters), BF),
            pltpu.VMEM((2 * filters, cells), BF),
        ],
        compiler_params=pltpu.CompilerParams(vmem_limit_bytes=16 * 1024 * 1024),
        cost_estimate=pl.CostEstimate(
            flops=6 * 27 * channels * filters * cells, bytes_accessed=2**21, transcendentals=0
        ),
        name="input_kernel",
    )(w, g0, g1, g2, g3)
    near, far, odd = swap_halo(to_above, to_below)
    weight_grad = gathered(piece)
    near = near.reshape(channels, planes, cols)
    far = far.reshape(channels, planes, cols)
    rims = jnp.stack([jnp.where(odd, near, far), jnp.where(odd, far, near)], axis=2)
    input_grad = core.reshape(inputs.shape) + rims
    weight_grad = weight_grad.reshape(3, 3, 3, channels, filters)
    return (input_grad, weight_grad)


def solution(mesh):
    return jax.shard_map(
        per_device,
        mesh=mesh,
        in_specs=(
            P("chan", None, "space", None),
            P("chan", None, "space", None),
            P(None, None, None, "chan", None),
        ),
        out_specs=(P("chan", None, "space", None), P(None, None, None, "chan", None)),
        check_vma=False,
    )
```
